32 devices in a mesh: region: 4 (over y, x), band: 8 (over z, core).
Axes of the slice: x: 2, y: 2, z: 4, core: 2. Of those that a mesh axis runs over, the one named last changes fastest.
Arguments:
- adjoint_in: float32 [128, 128, 512], P(None, 'band', 'region'), may hold values from -6 to 6
- courant_y: float32 [128, 128, 512], P(None, 'band', 'region'), may hold values from -0.45 to 0.45
- courant_x: float32 [128, 128, 512], P('band', None, 'region'), may hold values from -0.45 to 0.45
- diffusion_inverse: float32 [128, 128, 128], P('band')
- conv_weight: float32 [128, 512], P('band', 'region'), may hold values from 0.05 to 0.9
- cloud_base: int32 [128, 512], P('band', 'region'), may hold values from 0 to 63
- cloud_top: int32 [128, 512], P('band', 'region'), may hold values from 1 to 126, as said below
- sound_count: int32 [4, 64], P('region', 'band'), may hold values from 0 to 64, as said below
- xco2_adjoint: float32 [4, 64, 64], P('region', 'band'), may hold values from -6 to 6
- kernel: float32 [4, 64, 64, 128], P('region', 'band'), may hold values from 0.25 to 4
- sound_cols: int32 [4, 64, 64], P('region', 'band'), may hold values from 0 to 2047
Outputs:
- adjoint_out: float32 [128, 128, 512], P('band', None, 'region')
The draws below stay inside these ranges and needn't reach their ends.
Inputs may be any that keep to these rules, and one draw needn't show every extreme that they name: `sound_count`: in every region one destination band receives 64 live slots from every source band. `sound_cols`: several slots may name the same column; the column is the latitude row within the band times 128 plus the longitude within the region. cloud_top > cloud_base in every column.
All inputs are finite; a program needn't handle non-finite values.
Results may differ from the reference program's by a relative error of at most 0.00014.
Values sent between devices are 32-bit elements; how exact they have to be, the bound alone decides.
A program may use at most 64 MiB of HBM per device.

```python
import math
import jax
import jax.numpy as jnp
from jax import lax

LEV = 128
LAT_DEV = 16
LON_DEV = 128
SLOTS = 64
YSTEPS = 2
XSTEPS = 4
REGIONS = 4
BANDS = 8
LAT = 128
LON = 512


def cloud_levels(key):
    key_base, key_depth = jax.random.split(key)
    lowest = jax.random.randint(key_base, (LAT, LON), 0, LEV // 2, dtype=jnp.int32)
    cloud_depth = jax.random.randint(key_depth, (LAT, LON), 1, LEV // 2, dtype=jnp.int32)
    return (lowest, lowest + cloud_depth)


def draw_cloud_base(key, part):
    return cloud_levels(jax.random.fold_in(key, 17))[0]


def draw_cloud_top(key, part):
    return cloud_levels(jax.random.fold_in(key, 17))[1]


def draw_sound_count(key, part):
    key_count, key_busy = jax.random.split(jax.random.fold_in(key, 29))
    counts = jax.random.randint(key_count, (REGIONS, BANDS, BANDS), 0, SLOTS + 1, dtype=jnp.int32)
    busiest = jax.random.randint(key_busy, (REGIONS, 1, 1), 0, BANDS, dtype=jnp.int32)
    dest_band = jnp.arange(BANDS, dtype=jnp.int32)[None, None, :]
    counts = jnp.where(dest_band == busiest, SLOTS, counts)
    return counts.reshape(REGIONS, BANDS * BANDS)


def draw_diffusion_inverse(key, part):
    spread_part = jax.random.normal(key, (LAT, LEV, LEV), jnp.float32) * (0.5 / math.sqrt(LEV))
    levels = jnp.arange(LEV, dtype=jnp.int32)
    identity = (levels[:, None] == levels[None, :]).astype(jnp.float32)
    return identity[None] + spread_part


def plant(entries, stream_key, low, top_value):
    shape = entries.shape
    place = [jax.random.randint(jax.random.fold_in(stream_key, axis), (), 0, shape[axis]) for axis in range(len(shape))]
    entries = entries.at[tuple(place)].set(low)
    longest = shape.index(max(shape))
    place[longest] = (place[longest] + 1) % shape[longest]
    return entries.at[tuple(place)].set(top_value)


def steps_of(own_key, extent, cuts, low, largest):
    level, own = 1.0, jax.random.fold_in(own_key, 6)
    for dim, parts in cuts:
        steps = jnp.exp(jax.random.uniform(jax.random.fold_in(own, dim), (parts,), jnp.float32, low / len(cuts), largest / len(cuts)))
        level = level * jnp.repeat(steps, extent[dim] // parts).reshape([-1 if axis == dim else 1 for axis in range(len(extent))])
    return level


def noise(key, extent, width, most, pieces=(), kind=jnp.bfloat16):
    drawn = jax.random.normal(key, extent, jnp.float32) * width
    if len(pieces) > 0:
        drawn = steps_of(key, extent, pieces, -0.22, 0.18) * drawn
    return jnp.clip(drawn, min=-most, max=most).astype(kind)


def setup_inputs(seed: int = 0) -> dict:
    keys = jax.random.split(jax.random.key(seed), 12)
    return {
        "adjoint_in": noise(keys[0], (LEV, LAT, LON), 1.0, 6.0, ((1, 8), (2, 4)), jnp.float32),
        "courant_y": jnp.clip(jax.random.uniform(keys[1], (LEV, LAT, LON), jnp.float32, -0.45, 0.45) * steps_of(keys[1], (LEV, LAT, LON), ((1, 8), (2, 4)), -0.4, 0.0), -0.45, 0.45),
        "courant_x": jnp.clip(jax.random.uniform(keys[2], (LEV, LAT, LON), jnp.float32, -0.45, 0.45) * steps_of(keys[2], (LEV, LAT, LON), ((0, 8), (2, 4)), -0.4, 0.0), -0.45, 0.45),
        "diffusion_inverse": draw_diffusion_inverse(jax.random.fold_in(keys[11], 71), 0),
        "conv_weight": jnp.clip(jnp.exp(math.log(0.9) - 2.8903717 * jax.random.uniform(keys[4], (LAT, LON), jnp.float32) ** steps_of(keys[4], (LAT, LON), ((0, 8), (1, 4)), -0.2, 0.2)), 0.05, 0.9),
        "cloud_base": draw_cloud_base(jax.random.fold_in(keys[11], 71), 0),
        "cloud_top": draw_cloud_top(jax.random.fold_in(keys[11], 71), 0),
        "sound_count": draw_sound_count(jax.random.fold_in(keys[11], 71), 0),
        "xco2_adjoint": noise(keys[8], (REGIONS, BANDS * BANDS, SLOTS), 1.0, 6.0, ((0, 4), (1, 8)), jnp.float32),
        "kernel": jnp.clip(jnp.exp(math.log(4.0) - 2.7725887 * jax.random.uniform(keys[9], (REGIONS, BANDS * BANDS, SLOTS, LEV), jnp.float32) ** steps_of(keys[9], (REGIONS, BANDS * BANDS, SLOTS, LEV), ((0, 4), (1, 8)), -0.2, 0.2)), 0.25, 4.0),
        "sound_cols": plant(jax.random.randint(keys[10], (REGIONS, BANDS * BANDS, SLOTS), 0, LAT_DEV * LON_DEV), jax.random.fold_in(keys[10], 1), 0, (LAT_DEV * LON_DEV) - 1).astype(jnp.int32),
    }


def take_next(field, dim):
    kept_part = lax.slice_in_dim(field, 1, field.shape[dim], axis=dim)
    zero_edge = jnp.zeros_like(lax.slice_in_dim(field, 0, 1, axis=dim))
    return jnp.concatenate([kept_part, zero_edge], axis=dim)


def take_prev(field, dim):
    kept_part = lax.slice_in_dim(field, 0, field.shape[dim] - 1, axis=dim)
    zero_edge = jnp.zeros_like(lax.slice_in_dim(field, 0, 1, axis=dim))
    return jnp.concatenate([zero_edge, kept_part], axis=dim)


def advect_sweep(tracer, courant, dim):
    outflow_up = jnp.maximum(courant, 0.0)
    lower_prev = take_prev(jnp.minimum(courant, 0.0), dim)
    return (1.0 - outflow_up + lower_prev) * tracer + outflow_up * take_next(tracer, dim) - lower_prev * take_prev(tracer, dim)


def periodic_sweep(tracer, courant):
    outflow_up = jnp.maximum(courant, 0.0)
    lower_prev = jnp.roll(jnp.minimum(courant, 0.0), 1, axis=2)
    return (1.0 - outflow_up + lower_prev) * tracer + outflow_up * jnp.roll(tracer, -1, axis=2) - lower_prev * jnp.roll(tracer, 1, axis=2)


def convect(field, cloud_base, cloud_top, conv_weight):
    levels = jnp.arange(field.shape[0], dtype=jnp.int32)[:, None, None]
    inside = ((levels >= cloud_base[None]) & (levels <= cloud_top[None])).astype(field.dtype)
    cloud_depth = (cloud_top - cloud_base + 1).astype(field.dtype)
    column_mean = jnp.sum(inside * field, axis=0) / cloud_depth
    return field + conv_weight[None] * inside * (column_mean[None] - field)


def reference(adjoint_in, courant_y, courant_x, diffusion_inverse, conv_weight, cloud_base, cloud_top, sound_count, xco2_adjoint, kernel, sound_cols):
    slot_index = jnp.arange(SLOTS, dtype=jnp.int32)
    live_slot = slot_index[None, None, :] < sound_count[:, :, None]
    partial_value = jnp.where(live_slot, xco2_adjoint, jnp.zeros_like(xco2_adjoint))[..., None] * kernel
    partial_value = partial_value.reshape(REGIONS, BANDS, BANDS, SLOTS, LEV).transpose(0, 2, 1, 3, 4)
    slot_cols = sound_cols.reshape(REGIONS, BANDS, BANDS, SLOTS)
    region_index = jnp.arange(REGIONS, dtype=jnp.int32)[:, None, None, None]
    dest_band = jnp.arange(BANDS, dtype=jnp.int32)[None, :, None, None]
    lat_index = dest_band * LAT_DEV + slot_cols // LON_DEV
    lon_index = region_index * LON_DEV + slot_cols % LON_DEV
    flat_cols = (lat_index * LON + lon_index).reshape(-1).astype(jnp.int32)
    column = adjoint_in.reshape(LEV, LAT * LON)
    forced = column.at[:, flat_cols].add(partial_value.reshape(-1, LEV).T).reshape(LEV, LAT, LON)
    convected = convect(forced, cloud_base, cloud_top, conv_weight)
    tracer = jnp.einsum("jlk,lji->kji", diffusion_inverse, convected, precision=lax.Precision.HIGHEST)
    rows = jnp.arange(LAT, dtype=jnp.int32)[None, :, None]
    courant_eff = jnp.where(rows < LAT - 1, courant_y, jnp.zeros_like(courant_y))
    for substep in range(YSTEPS):
        tracer = advect_sweep(tracer, courant_eff, 1)
    for substep in range(XSTEPS):
        tracer = periodic_sweep(tracer, courant_x)
    return tracer
```

```python
import functools

import jax
import jax.numpy as jnp
from jax import lax
from jax.experimental import pallas as pl
from jax.experimental.pallas import tpu as pltpu
from jax.sharding import PartitionSpec as P

XSTEPS = 4
PACK = 2 * XSTEPS
F32 = jnp.float32
BF16 = jnp.bfloat16


def split(x):
    hi = x.astype(BF16)
    return hi, (x - hi.astype(F32)).astype(BF16)


def step_kernel(
    nb, nr, lev, jb, ln, slots,
    adj, cy, cx, diff, conv_weight, base, top, count, xco2, kern, cols,
    out,
    ps, pr, onehot, ptb, dtb, mixed, mix_halo, cy_send, cy_halo,
    outgoing, arrived, cpack, cleft, cright, xpack, xleft, xright,
    s_send, s_recv, a_send, a_recv, h_send, h_recv, c_send, c_recv,
    l_send, l_recv, r_send, r_recv,
):
    lanes = 128
    n = ln * jb
    groups = lanes // PACK
    q = n // groups
    me = lax.axis_index("band")
    reg = lax.axis_index("region")
    right = lax.rem(reg + 1, nr)
    left = lax.rem(reg + nr - 1, nr)

    def partner(t):
        d, bit = 0, 1
        while bit < nb:
            d = d + bit * (((me // bit) % 2 + (t // bit) % 2) % 2)
            bit *= 2
        return d

    def to_band(src, dst, s_sem, r_sem, d):
        return pltpu.make_async_remote_copy(
            src_ref=src, dst_ref=dst, send_sem=s_sem, recv_sem=r_sem,
            device_id=(reg, d), device_id_type=pl.DeviceIdType.MESH)

    def to_region(src, dst, s_sem, r_sem, r):
        return pltpu.make_async_remote_copy(
            src_ref=src, dst_ref=dst, send_sem=s_sem, recv_sem=r_sem,
            device_id=(r, me), device_id_type=pl.DeviceIdType.MESH)

    barrier = pltpu.get_barrier_semaphore()
    for t in range(1, nb):
        pl.semaphore_signal(barrier, inc=1, device_id=(reg, partner(t)),
                            device_id_type=pl.DeviceIdType.MESH)
    for r in (left, right):
        pl.semaphore_signal(barrier, inc=1, device_id=(r, me),
                            device_id_type=pl.DeviceIdType.MESH)

    lane_row = lax.broadcasted_iota(jnp.int32, (1, slots), 1)
    eye = (lax.broadcasted_iota(jnp.int32, (slots, slots), 0)
           == lax.broadcasted_iota(jnp.int32, (slots, slots), 1))

    def as_column(row):
        return jnp.sum(jnp.where(eye, row, 0.0), axis=1, keepdims=True)

    for d in range(nb):
        w = jnp.where(lane_row < count[0, d], xco2[0, d:d + 1, :], 0.0)
        ps[d] = as_column(w) * kern[0, d]
    pr[me] = ps[me]

    pl.semaphore_wait(barrier, nb + 1)

    def sounding_copy(t):
        d = partner(t)
        return to_band(ps.at[d], pr.at[me], s_send.at[t], s_recv.at[t], d)

    for t in range(nb - 1, 0, -1):
        sounding_copy(t).start()

    cy_send[0] = cy[pl.ds(jb - 2, lev, stride=jb), :]
    cy_send[1] = cy[pl.ds(jb - 1, lev, stride=jb), :]
    cy_send[2] = cy[pl.ds(0, lev, stride=jb), :]

    def cy_up():
        return to_band(cy_send.at[pl.ds(0, 2)], cy_halo.at[pl.ds(0, 2)], h_send.at[0], h_recv.at[0], me + 1)

    def cy_down():
        return to_band(cy_send.at[pl.ds(2, 1)], cy_halo.at[pl.ds(2, 1)], h_send.at[1], h_recv.at[1], me - 1)

    def mix_up():
        return to_band(mixed.at[pl.ds(jb - 2, 2)], mix_halo.at[pl.ds(0, 2)], h_send.at[2], h_recv.at[2], me + 1)

    def mix_down():
        return to_band(mixed.at[pl.ds(0, 2)], mix_halo.at[pl.ds(2, 2)], h_send.at[3], h_recv.at[3], me - 1)

    has_next = me < nb - 1
    has_prev = me > 0

    @pl.when(has_next)
    def _():
        cy_up().start()

    @pl.when(has_prev)
    def _():
        cy_down().start()

    @pl.when(me == 0)
    def _():
        mix_halo[0:2] = jnp.zeros((2, lev, lanes), F32)
        cy_halo[0:2] = jnp.zeros((2, lev, lanes), F32)

    @pl.when(me == nb - 1)
    def _():
        mix_halo[2:4] = jnp.zeros((2, lev, lanes), F32)
        cy_halo[2:3] = jnp.zeros((1, lev, lanes), F32)

    lane = lax.broadcasted_iota(jnp.int32, (q, lanes), 1)
    lane_in = lane % PACK

    def pack(rows):
        total = jnp.zeros((q, lanes), F32)
        for g in range(groups):
            moved = pltpu.roll(rows(g), (XSTEPS + PACK * g) % lanes, 1)
            total = jnp.where(lane // PACK == g, moved, total)
        return total

    def cx_rows(s, g):
        k, jo = (g * q) // jb, (g * q) % jb
        return cx[k, pl.ds(pl.multiple_of(s * jb + jo, 8), q), :]

    def pack_courant(s, carry):
        cpack[s] = pack(lambda g: cx_rows(s, g))
        return carry

    lax.fori_loop(0, nb, pack_courant, 0)
    c_right = to_region(cpack, cleft, c_send.at[0], c_recv.at[0], right)
    c_left = to_region(cpack, cright, c_send.at[1], c_recv.at[1], left)
    c_right.start()
    c_left.start()

    cell = lax.broadcasted_iota(jnp.int32, (slots, lanes), 1).astype(F32)
    for s in range(nb):
        col = as_column(cols[0, s:s + 1, :].astype(F32))
        for j in range(jb):
            hit = jnp.where(col == cell + float(j * lanes), 1.0, 0.0)
            onehot[s * slots:(s + 1) * slots, j * lanes:(j + 1) * lanes] = hit.astype(BF16)

    def split_mix(j, carry):
        hi, lo = split(diff[j].T)
        dtb[j, :, 0:lev] = hi
        dtb[j, :, lev:2 * lev] = lo
        dtb[j, :, 2 * lev:3 * lev] = hi
        return carry

    lax.fori_loop(0, jb, split_mix, 0)

    for t in range(nb - 1, 0, -1):
        sounding_copy(t).wait_recv()
    for s in range(nb):
        hi, lo = split(pr[s].T)
        ptb[0:lev, s * slots:(s + 1) * slots] = hi
        ptb[lev:2 * lev, s * slots:(s + 1) * slots] = lo

    level = lax.broadcasted_iota(jnp.int32, (lev, lanes), 0)

    def mix_pair(jp):
        both = jnp.dot(ptb[...], onehot[:, pl.ds(pl.multiple_of(jp * 2 * lanes, 2 * lanes), 2 * lanes)],
                       preferred_element_type=F32)
        add = both[0:lev] + both[lev:2 * lev]
        for h in range(2):
            j = jp * 2 + h
            forced = adj[pl.ds(j, lev, stride=jb), :] + add[:, h * lanes:(h + 1) * lanes]
            lowest, highest = base[pl.ds(j, 1), :], top[pl.ds(j, 1), :]
            inside = (level >= lowest) & (level <= highest)
            depth = (highest - lowest + 1).astype(F32)
            mean = jnp.sum(jnp.where(inside, forced, 0.0), axis=0, keepdims=True) / depth
            conv = forced + jnp.where(inside, conv_weight[pl.ds(j, 1), :] * (mean - forced), 0.0)
            hi, lo = split(conv)
            mixed[j] = jnp.dot(dtb[j], jnp.concatenate([hi, hi, lo], axis=0), preferred_element_type=F32)

    mix_pair(0)

    @pl.when(has_prev)
    def _():
        mix_down().start()

    mix_pair(jb // 2 - 1)

    @pl.when(has_next)
    def _():
        mix_up().start()

    def mix_rest(jp, carry):
        mix_pair(jp)
        return carry

    lax.fori_loop(1, jb // 2 - 1, mix_rest, 0)

    @pl.when(has_next)
    def _():
        cy_down().wait_recv()
        mix_down().wait_recv()

    @pl.when(has_prev)
    def _():
        cy_up().wait_recv()
        mix_up().wait_recv()

    def sweep_y(d, store):
        ls = pl.ds(pl.multiple_of(d * ln, 8), ln)

        def field(r):
            if r < 2:
                return mix_halo[r, ls, :]
            if r < jb + 2:
                return mixed[r - 2, ls, :]
            return mix_halo[r - jb, ls, :]

        def courant(r):
            if r < 2:
                return cy_halo[r, ls, :]
            if r < jb + 2:
                c = cy[pl.ds(d * n + (r - 2), ln, stride=jb), :]
                return jnp.where(has_next, c, 0.0) if r == jb + 1 else c
            return cy_halo[2, ls, :]

        c_prev = jnp.minimum(courant(0), 0.0)
        a_prev, a_here = field(0), field(1)
        b_back = b_here = None
        coef = []
        for r in range(1, jb + 3):
            c_here = courant(r)
            a_next = field(r + 1)
            up = jnp.maximum(c_here, 0.0)
            mid = 1.0 - up + c_prev
            b_next = mid * a_here + up * a_next - c_prev * a_prev
            coef.append((mid, up, c_prev))
            if r >= 3:
                m2, u2, p2 = coef[-2]
                store(r - 3, m2 * b_here + u2 * b_next - p2 * b_back)
            b_back, b_here = b_here, b_next
            a_prev, a_here = a_here, a_next
            c_prev = jnp.minimum(c_here, 0.0)

    def block_copy(t):
        d = partner(t)
        return to_band(outgoing.at[pl.ds(pl.multiple_of(t * n, 8), n)],
                       arrived.at[pl.ds(pl.multiple_of(me * n, 8), n)],
                       a_send.at[t], a_recv.at[t], d)

    def send_block(i, carry):
        t = nb - 1 - i

        def store(j, value):
            outgoing[pl.ds(t * n + j, ln, stride=jb), :] = value

        sweep_y(partner(t), store)
        block_copy(t).start()
        return carry

    lax.fori_loop(0, nb - 1, send_block, 0)

    def store_own(j, value):
        arrived[pl.ds(me * n + j, ln, stride=jb), :] = value

    sweep_y(me, store_own)

    def halo_right(t):
        s = partner(t)
        return to_region(xpack.at[s], xleft.at[s], r_send.at[t], r_recv.at[t], right)

    def halo_left(t):
        s = partner(t)
        return to_region(xpack.at[s], xright.at[s], l_send.at[t], l_recv.at[t], left)

    def prepare(t):
        s = partner(t)
        xpack[s] = pack(lambda g: arrived[pl.ds(pl.multiple_of(s * n + g * q, 8), q), :])
        halo_right(t).start()
        halo_left(t).start()

    def finish(t):
        s = partner(t)
        halo_right(t).wait_recv()
        halo_left(t).wait_recv()
        low = lane_in < XSTEPS
        own, c_own = xpack[s], cpack[s]
        a = jnp.where(low, xleft[s], own)
        b = jnp.where(low, own, xright[s])
        ca = jnp.where(low, cleft[s], c_own)
        cb = jnp.where(low, c_own, cright[s])

        def coefs(c):
            up = jnp.maximum(c, 0.0)
            low_prev = pltpu.roll(jnp.minimum(c, 0.0), 1, 1)
            return 1.0 - up + low_prev, up, low_prev

        za, pa, ma = coefs(ca)
        zb, pb, mb = coefs(cb)
        edges = []
        for step in range(XSTEPS):
            a_prev, b_next = pltpu.roll(a, 1, 1), pltpu.roll(b, lanes - 1, 1)
            edges.append(jnp.where(lane_in == XSTEPS, a_prev, b_next))
            if step < XSTEPS - 1:
                a = za * a + pa * pltpu.roll(a, lanes - 1, 1) - ma * a_prev
                b = zb * b + pb * b_next - mb * pltpu.roll(b, 1, 1)
        first, last = lane == 0, lane == lanes - 1
        for g in range(groups):
            back = (lanes - XSTEPS - PACK * g) % lanes
            x = arrived[pl.ds(pl.multiple_of(s * n + g * q, 8), q), :]
            c = cx_rows(s, g)
            up = jnp.maximum(c, 0.0)
            low_prev = jnp.where(first, pltpu.roll(ma, back, 1), pltpu.roll(jnp.minimum(c, 0.0), 1, 1))
            mid = 1.0 - up + low_prev
            for step in range(XSTEPS):
                edge = pltpu.roll(edges[step], back, 1)
                nxt = jnp.where(last, edge, pltpu.roll(x, lanes - 1, 1))
                prv = jnp.where(first, edge, pltpu.roll(x, 1, 1))
                x = mid * x + up * nxt - low_prev * prv
            k, jo = (g * q) // jb, (g * q) % jb
            out[k, pl.ds(pl.multiple_of(s * jb + jo, 8), q), :] = x

    prepare(0)
    c_right.wait_recv()
    c_left.wait_recv()

    def drain(i, carry):
        t = nb - i
        block_copy(t).wait_recv()
        prepare(t)
        finish((t + 1) % nb)
        return carry

    lax.fori_loop(1, nb, drain, 0)
    finish(1)

    c_right.wait_send()
    c_left.wait_send()

    @pl.when(has_next)
    def _():
        cy_up().wait_send()
        mix_up().wait_send()

    @pl.when(has_prev)
    def _():
        cy_down().wait_send()
        mix_down().wait_send()

    def finish_sends(t, carry):
        halo_right(t).wait_send()
        halo_left(t).wait_send()
        return carry

    lax.fori_loop(0, nb, finish_sends, 0)

    def finish_blocks(t, carry):
        sounding_copy(t).wait_send()
        block_copy(t).wait_send()
        return carry

    lax.fori_loop(1, nb, finish_blocks, 0)


def per_device(nb, nr, adj, cy, cx, diff, conv_weight, base, top, count, xco2, kern, cols):
    lev, jb, lanes = adj.shape
    ln, lat, _ = cx.shape
    slots = kern.shape[2]
    n = ln * jb
    q = n * PACK // lanes
    vmem = pl.BlockSpec(memory_space=pltpu.VMEM)
    smem = pl.BlockSpec(memory_space=pltpu.SMEM)
    dma = pltpu.SemaphoreType.DMA
    rows = (nb, q, lanes)
    return pl.pallas_call(
        functools.partial(step_kernel, nb, nr, lev, jb, ln, slots),
        out_shape=jax.ShapeDtypeStruct((ln, lat, lanes), F32),
        in_specs=[vmem] * 7 + [smem] + [vmem] * 3,
        out_specs=vmem,
        scratch_shapes=[
            pltpu.VMEM((nb, slots, lev), F32),
            pltpu.VMEM((nb, slots, lev), F32),
            pltpu.VMEM((nb * slots, jb * lanes), BF16),
            pltpu.VMEM((2 * lev, nb * slots), BF16),
            pltpu.VMEM((jb, lev, 3 * lev), BF16),
            pltpu.VMEM((jb, lev, lanes), F32),
            pltpu.VMEM((4, lev, lanes), F32),
            pltpu.VMEM((3, lev, lanes), F32),
            pltpu.VMEM((3, lev, lanes), F32),
            pltpu.VMEM((nb * n, lanes), F32),
            pltpu.VMEM((nb * n, lanes), F32),
            pltpu.VMEM(rows, F32), pltpu.VMEM(rows, F32), pltpu.VMEM(rows, F32),
            pltpu.VMEM(rows, F32), pltpu.VMEM(rows, F32), pltpu.VMEM(rows, F32),
            dma((nb,)), dma((nb,)), dma((nb,)), dma((nb,)),
            dma((4,)), dma((4,)), dma((2,)), dma((2,)),
            dma((nb,)), dma((nb,)), dma((nb,)), dma((nb,)),
        ],
        compiler_params=pltpu.CompilerParams(
            collective_id=0, has_side_effects=True, vmem_limit_bytes=48 * 1024 * 1024),
    )(adj.reshape(lev * jb, lanes), cy.reshape(lev * jb, lanes), cx, diff,
      conv_weight, base, top, count, xco2, kern, cols)


def solution(mesh):
    in_specs = (
        P(None, "band", "region"),
        P(None, "band", "region"),
        P("band", None, "region"),
        P("band", None, None),
        P("band", "region"),
        P("band", "region"),
        P("band", "region"),
        P("region", "band"),
        P("region", "band", None),
        P("region", "band", None, None),
        P("region", "band", None),
    )
    run = functools.partial(per_device, mesh.shape["band"], mesh.shape["region"])
    return jax.shard_map(
        run, mesh=mesh, in_specs=in_specs, out_specs=P("band", None, "region"), check_vma=False
    )
```

```python
import functools

import jax
import jax.numpy as jnp
from jax import lax
from jax.experimental import pallas as pl
from jax.experimental.pallas import tpu as pltpu
from jax.sharding import PartitionSpec as P

XSTEPS = 4
PACK = 2 * XSTEPS
F32 = jnp.float32
BF16 = jnp.bfloat16


def split(x):
    hi = x.astype(BF16)
    return hi, (x - hi.astype(F32)).astype(BF16)


def step_kernel(
    nb, nr, lev, jb, ln, slots,
    adj_hbm, cy_hbm, cx_hbm, diff_hbm, conv_hbm, base_hbm, top_hbm, count_hbm, xco2_hbm, kern_hbm, cols_hbm,
    out,
    adj, cy, cx, diff, conv_weight, base, top, count, xco2, kern, cols, in_sem,
    ps, pr, onehot, ptb, dtb, mixed, mix_halo, cy_send, cy_halo,
    outgoing, arrived, cpack, cleft, cright, xpack, xleft, xright,
    s_send, s_recv, a_send, a_recv, h_send, h_recv, c_send, c_recv,
    l_send, l_recv, r_send, r_recv,
):
    lanes = 128
    n = ln * jb
    loads = {}
    for slot, (name, src, dst) in enumerate((
        ("kern", kern_hbm, kern), ("xco2", xco2_hbm, xco2), ("count", count_hbm, count),
        ("cy", cy_hbm, cy), ("cx", cx_hbm, cx), ("cols", cols_hbm, cols), ("diff", diff_hbm, diff),
        ("adj", adj_hbm, adj), ("conv", conv_hbm, conv_weight), ("base", base_hbm, base), ("top", top_hbm, top),
    )):
        loads[name] = pltpu.make_async_copy(src, dst, in_sem.at[slot])
        loads[name].start()
    groups = lanes // PACK
    q = n // groups
    me = lax.axis_index("band")
    reg = lax.axis_index("region")
    right = lax.rem(reg + 1, nr)
    left = lax.rem(reg + nr - 1, nr)

    def partner(t):
        d, bit = 0, 1
        while bit < nb:
            d = d + bit * (((me // bit) % 2 + (t // bit) % 2) % 2)
            bit *= 2
        return d

    def to_band(src, dst, s_sem, r_sem, d):
        return pltpu.make_async_remote_copy(
            src_ref=src, dst_ref=dst, send_sem=s_sem, recv_sem=r_sem,
            device_id=(reg, d), device_id_type=pl.DeviceIdType.MESH)

    def to_region(src, dst, s_sem, r_sem, r):
        return pltpu.make_async_remote_copy(
            src_ref=src, dst_ref=dst, send_sem=s_sem, recv_sem=r_sem,
            device_id=(r, me), device_id_type=pl.DeviceIdType.MESH)

    barrier = pltpu.get_barrier_semaphore()
    for t in range(1, nb):
        pl.semaphore_signal(barrier, inc=1, device_id=(reg, partner(t)),
                            device_id_type=pl.DeviceIdType.MESH)
    for r in (left, right):
        pl.semaphore_signal(barrier, inc=1, device_id=(r, me),
                            device_id_type=pl.DeviceIdType.MESH)

    lane_row = lax.broadcasted_iota(jnp.int32, (1, slots), 1)
    eye = (lax.broadcasted_iota(jnp.int32, (slots, slots), 0)
           == lax.broadcasted_iota(jnp.int32, (slots, slots), 1))

    def as_column(row):
        return jnp.sum(jnp.where(eye, row, 0.0), axis=1, keepdims=True)

    for name in ("kern", "xco2", "count"):
        loads[name].wait()

    for d in range(nb):
        w = jnp.where(lane_row < count[0:1, d:d + 1], xco2[0, d:d + 1, :], 0.0)
        ps[d] = as_column(w) * kern[0, d]
    pr[me] = ps[me]

    pl.semaphore_wait(barrier, nb + 1)

    def sounding_copy(t):
        d = partner(t)
        return to_band(ps.at[d], pr.at[me], s_send.at[t], s_recv.at[t], d)

    for t in range(nb - 1, 0, -1):
        sounding_copy(t).start()

    loads["cy"].wait()

    cy_send[0] = cy[pl.ds(jb - 2, lev, stride=jb), :]
    cy_send[1] = cy[pl.ds(jb - 1, lev, stride=jb), :]
    cy_send[2] = cy[pl.ds(0, lev, stride=jb), :]

    def cy_up():
        return to_band(cy_send.at[pl.ds(0, 2)], cy_halo.at[pl.ds(0, 2)], h_send.at[0], h_recv.at[0], me + 1)

    def cy_down():
        return to_band(cy_send.at[pl.ds(2, 1)], cy_halo.at[pl.ds(2, 1)], h_send.at[1], h_recv.at[1], me - 1)

    def mix_up():
        return to_band(mixed.at[pl.ds(jb - 2, 2)], mix_halo.at[pl.ds(0, 2)], h_send.at[2], h_recv.at[2], me + 1)

    def mix_down():
        return to_band(mixed.at[pl.ds(0, 2)], mix_halo.at[pl.ds(2, 2)], h_send.at[3], h_recv.at[3], me - 1)

    has_next = me < nb - 1
    has_prev = me > 0

    @pl.when(has_next)
    def _():
        cy_up().start()

    @pl.when(has_prev)
    def _():
        cy_down().start()

    @pl.when(me == 0)
    def _():
        mix_halo[0:2] = jnp.zeros((2, lev, lanes), F32)
        cy_halo[0:2] = jnp.zeros((2, lev, lanes), F32)

    @pl.when(me == nb - 1)
    def _():
        mix_halo[2:4] = jnp.zeros((2, lev, lanes), F32)
        cy_halo[2:3] = jnp.zeros((1, lev, lanes), F32)

    lane = lax.broadcasted_iota(jnp.int32, (q, lanes), 1)
    lane_in = lane % PACK

    def pack(rows):
        total = jnp.zeros((q, lanes), F32)
        for g in range(groups):
            moved = pltpu.roll(rows(g), (XSTEPS + PACK * g) % lanes, 1)
            total = jnp.where(lane // PACK == g, moved, total)
        return total

    def cx_rows(s, g):
        k, jo = (g * q) // jb, (g * q) % jb
        return cx[k, pl.ds(pl.multiple_of(s * jb + jo, 8), q), :]

    def pack_courant(s, carry):
        cpack[s] = pack(lambda g: cx_rows(s, g))
        return carry

    loads["cx"].wait()
    lax.fori_loop(0, nb, pack_courant, 0)
    c_right = to_region(cpack, cleft, c_send.at[0], c_recv.at[0], right)
    c_left = to_region(cpack, cright, c_send.at[1], c_recv.at[1], left)
    c_right.start()
    c_left.start()

    loads["cols"].wait()
    loads["diff"].wait()

    cell = lax.broadcasted_iota(jnp.int32, (slots, lanes), 1).astype(F32)
    for s in range(nb):
        col = as_column(cols[0, s:s + 1, :].astype(F32))
        for j in range(jb):
            hit = jnp.where(col == cell + float(j * lanes), 1.0, 0.0)
            onehot[s * slots:(s + 1) * slots, j * lanes:(j + 1) * lanes] = hit.astype(BF16)

    def split_mix(j, carry):
        hi, lo = split(diff[j].T)
        dtb[j, :, 0:lev] = hi
        dtb[j, :, lev:2 * lev] = lo
        dtb[j, :, 2 * lev:3 * lev] = hi
        return carry

    lax.fori_loop(0, jb, split_mix, 0)

    for t in range(nb - 1, 0, -1):
        sounding_copy(t).wait_recv()
    for s in range(nb):
        hi, lo = split(pr[s].T)
        ptb[0:lev, s * slots:(s + 1) * slots] = hi
        ptb[lev:2 * lev, s * slots:(s + 1) * slots] = lo

    for name in ("adj", "conv", "base", "top"):
        loads[name].wait()

    level = lax.broadcasted_iota(jnp.int32, (lev, lanes), 0)

    def mix_pair(jp):
        both = jnp.dot(ptb[...], onehot[:, pl.ds(pl.multiple_of(jp * 2 * lanes, 2 * lanes), 2 * lanes)],
                       preferred_element_type=F32)
        add = both[0:lev] + both[lev:2 * lev]
        for h in range(2):
            j = jp * 2 + h
            forced = adj[pl.ds(j, lev, stride=jb), :] + add[:, h * lanes:(h + 1) * lanes]
            lowest, highest = base[pl.ds(j, 1), :], top[pl.ds(j, 1), :]
            inside = (level >= lowest) & (level <= highest)
            depth = (highest - lowest + 1).astype(F32)
            mean = jnp.sum(jnp.where(inside, forced, 0.0), axis=0, keepdims=True) / depth
            conv = forced + jnp.where(inside, conv_weight[pl.ds(j, 1), :] * (mean - forced), 0.0)
            hi, lo = split(conv)
            mixed[j] = jnp.dot(dtb[j], jnp.concatenate([hi, hi, lo], axis=0), preferred_element_type=F32)

    mix_pair(0)

    @pl.when(has_prev)
    def _():
        mix_down().start()

    mix_pair(jb // 2 - 1)

    @pl.when(has_next)
    def _():
        mix_up().start()

    def mix_rest(jp, carry):
        mix_pair(jp)
        return carry

    lax.fori_loop(1, jb // 2 - 1, mix_rest, 0)

    @pl.when(has_next)
    def _():
        cy_down().wait_recv()
        mix_down().wait_recv()

    @pl.when(has_prev)
    def _():
        cy_up().wait_recv()
        mix_up().wait_recv()

    def sweep_y(d, store):
        ls = pl.ds(pl.multiple_of(d * ln, 8), ln)

        def field(r):
            if r < 2:
                return mix_halo[r, ls, :]
            if r < jb + 2:
                return mixed[r - 2, ls, :]
            return mix_halo[r - jb, ls, :]

        def courant(r):
            if r < 2:
                return cy_halo[r, ls, :]
            if r < jb + 2:
                c = cy[pl.ds(d * n + (r - 2), ln, stride=jb), :]
                return jnp.where(has_next, c, 0.0) if r == jb + 1 else c
            return cy_halo[2, ls, :]

        c_prev = jnp.minimum(courant(0), 0.0)
        a_prev, a_here = field(0), field(1)
        b_back = b_here = None
        coef = []
        for r in range(1, jb + 3):
            c_here = courant(r)
            a_next = field(r + 1)
            up = jnp.maximum(c_here, 0.0)
            mid = 1.0 - up + c_prev
            b_next = mid * a_here + up * a_next - c_prev * a_prev
            coef.append((mid, up, c_prev))
            if r >= 3:
                m2, u2, p2 = coef[-2]
                store(r - 3, m2 * b_here + u2 * b_next - p2 * b_back)
            b_back, b_here = b_here, b_next
            a_prev, a_here = a_here, a_next
            c_prev = jnp.minimum(c_here, 0.0)

    def block_copy(t):
        d = partner(t)
        return to_band(outgoing.at[pl.ds(pl.multiple_of(t * n, 8), n)],
                       arrived.at[pl.ds(pl.multiple_of(me * n, 8), n)],
                       a_send.at[t], a_recv.at[t], d)

    def send_block(i, carry):
        t = nb - 1 - i

        def store(j, value):
            outgoing[pl.ds(t * n + j, ln, stride=jb), :] = value

        sweep_y(partner(t), store)
        block_copy(t).start()
        return carry

    lax.fori_loop(0, nb - 1, send_block, 0)

    def store_own(j, value):
        arrived[pl.ds(me * n + j, ln, stride=jb), :] = value

    sweep_y(me, store_own)

    def halo_right(t):
        s = partner(t)
        return to_region(xpack.at[s], xleft.at[s], r_send.at[t], r_recv.at[t], right)

    def halo_left(t):
        s = partner(t)
        return to_region(xpack.at[s], xright.at[s], l_send.at[t], l_recv.at[t], left)

    def prepare(t):
        s = partner(t)
        xpack[s] = pack(lambda g: arrived[pl.ds(pl.multiple_of(s * n + g * q, 8), q), :])
        halo_right(t).start()
        halo_left(t).start()

    def finish(t):
        s = partner(t)
        halo_right(t).wait_recv()
        halo_left(t).wait_recv()
        low = lane_in < XSTEPS
        own, c_own = xpack[s], cpack[s]
        a = jnp.where(low, xleft[s], own)
        b = jnp.where(low, own, xright[s])
        ca = jnp.where(low, cleft[s], c_own)
        cb = jnp.where(low, c_own, cright[s])

        def coefs(c):
            up = jnp.maximum(c, 0.0)
            low_prev = pltpu.roll(jnp.minimum(c, 0.0), 1, 1)
            return 1.0 - up + low_prev, up, low_prev

        za, pa, ma = coefs(ca)
        zb, pb, mb = coefs(cb)
        edges = []
        for step in range(XSTEPS):
            a_prev, b_next = pltpu.roll(a, 1, 1), pltpu.roll(b, lanes - 1, 1)
            edges.append(jnp.where(lane_in == XSTEPS, a_prev, b_next))
            if step < XSTEPS - 1:
                a = za * a + pa * pltpu.roll(a, lanes - 1, 1) - ma * a_prev
                b = zb * b + pb * b_next - mb * pltpu.roll(b, 1, 1)
        first, last = lane == 0, lane == lanes - 1
        for g in range(groups):
            back = (lanes - XSTEPS - PACK * g) % lanes
            x = arrived[pl.ds(pl.multiple_of(s * n + g * q, 8), q), :]
            c = cx_rows(s, g)
            up = jnp.maximum(c, 0.0)
            low_prev = jnp.where(first, pltpu.roll(ma, back, 1), pltpu.roll(jnp.minimum(c, 0.0), 1, 1))
            mid = 1.0 - up + low_prev
            for step in range(XSTEPS):
                edge = pltpu.roll(edges[step], back, 1)
                nxt = jnp.where(last, edge, pltpu.roll(x, lanes - 1, 1))
                prv = jnp.where(first, edge, pltpu.roll(x, 1, 1))
                x = mid * x + up * nxt - low_prev * prv
            k, jo = (g * q) // jb, (g * q) % jb
            out[k, pl.ds(pl.multiple_of(s * jb + jo, 8), q), :] = x

    prepare(0)
    c_right.wait_recv()
    c_left.wait_recv()

    def drain(i, carry):
        block_copy(i).wait_recv()
        prepare(i)
        finish(i - 1)
        return carry

    lax.fori_loop(1, nb, drain, 0)
    finish(nb - 1)

    c_right.wait_send()
    c_left.wait_send()

    @pl.when(has_next)
    def _():
        cy_up().wait_send()
        mix_up().wait_send()

    @pl.when(has_prev)
    def _():
        cy_down().wait_send()
        mix_down().wait_send()

    def finish_sends(t, carry):
        halo_right(t).wait_send()
        halo_left(t).wait_send()
        return carry

    lax.fori_loop(0, nb, finish_sends, 0)

    def finish_blocks(t, carry):
        sounding_copy(t).wait_send()
        block_copy(t).wait_send()
        return carry

    lax.fori_loop(1, nb, finish_blocks, 0)


def per_device(nb, nr, adj, cy, cx, diff, conv_weight, base, top, count, xco2, kern, cols):
    lev, jb, lanes = adj.shape
    ln, lat, _ = cx.shape
    slots = kern.shape[2]
    n = ln * jb
    q = n * PACK // lanes
    vmem = pl.BlockSpec(memory_space=pltpu.VMEM)
    hbm = pl.BlockSpec(memory_space=pltpu.HBM)
    operands = (adj.reshape(lev * jb, lanes), cy.reshape(lev * jb, lanes), cx, diff,
                conv_weight, base, top, count, xco2, kern, cols)
    dma = pltpu.SemaphoreType.DMA
    rows = (nb, q, lanes)
    return pl.pallas_call(
        functools.partial(step_kernel, nb, nr, lev, jb, ln, slots),
        out_shape=jax.ShapeDtypeStruct((ln, lat, lanes), F32),
        in_specs=[hbm] * len(operands),
        out_specs=vmem,
        scratch_shapes=[pltpu.VMEM(x.shape, x.dtype) for x in operands] + [
            dma((len(operands),)),
            pltpu.VMEM((nb, slots, lev), F32),
            pltpu.VMEM((nb, slots, lev), F32),
            pltpu.VMEM((nb * slots, jb * lanes), BF16),
            pltpu.VMEM((2 * lev, nb * slots), BF16),
            pltpu.VMEM((jb, lev, 3 * lev), BF16),
            pltpu.VMEM((jb, lev, lanes), F32),
            pltpu.VMEM((4, lev, lanes), F32),
            pltpu.VMEM((3, lev, lanes), F32),
            pltpu.VMEM((3, lev, lanes), F32),
            pltpu.VMEM((nb * n, lanes), F32),
            pltpu.VMEM((nb * n, lanes), F32),
            pltpu.VMEM(rows, F32), pltpu.VMEM(rows, F32), pltpu.VMEM(rows, F32),
            pltpu.VMEM(rows, F32), pltpu.VMEM(rows, F32), pltpu.VMEM(rows, F32),
            dma((nb,)), dma((nb,)), dma((nb,)), dma((nb,)),
            dma((4,)), dma((4,)), dma((2,)), dma((2,)),
            dma((nb,)), dma((nb,)), dma((nb,)), dma((nb,)),
        ],
        compiler_params=pltpu.CompilerParams(
            collective_id=0, has_side_effects=True, vmem_limit_bytes=63 * 1024 * 1024),
    )(*operands)


def solution(mesh):
    in_specs = (
        P(None, "band", "region"),
        P(None, "band", "region"),
        P("band", None, "region"),
        P("band", None, None),
        P("band", "region"),
        P("band", "region"),
        P("band", "region"),
        P("region", "band"),
        P("region", "band", None),
        P("region", "band", None, None),
        P("region", "band", None),
    )
    run = functools.partial(per_device, mesh.shape["band"], mesh.shape["region"])
    return jax.shard_map(
        run, mesh=mesh, in_specs=in_specs, out_specs=P("band", None, "region"), check_vma=False
    )
```

```python
import functools

import jax
import jax.numpy as jnp
from jax import lax
from jax.experimental import pallas as pl
from jax.experimental.pallas import tpu as pltpu
from jax.sharding import PartitionSpec as P

XSTEPS = 4
PACK = 2 * XSTEPS
LAG = 2
F32 = jnp.float32
BF16 = jnp.bfloat16


def split(x):
    hi = x.astype(BF16)
    return hi, (x - hi.astype(F32)).astype(BF16)


def step_kernel(
    nb, nr, lev, jb, ln, slots,
    adj_hbm, cy_hbm, cx_hbm, diff_hbm, conv_hbm, base_hbm, top_hbm, count_hbm, xco2_hbm, kern_hbm, cols_hbm,
    out,
    adj, cy, cx, diff, conv_weight, base, top, count, xco2, kern, cols, in_sem,
    ps, pr, onehot, ptb, dtb, mixed, mix_halo, cy_send, cy_halo,
    outgoing, arrived, cpack, cleft, cright, xpack, xleft, xright,
    s_send, s_recv, a_send, a_recv, h_send, h_recv, c_send, c_recv,
    l_send, l_recv, r_send, r_recv,
):
    lanes = 128
    n = ln * jb
    loads = {}
    for slot, (name, src, dst) in enumerate((
        ("kern", kern_hbm, kern), ("xco2", xco2_hbm, xco2), ("count", count_hbm, count),
        ("cy", cy_hbm, cy), ("cx", cx_hbm, cx), ("cols", cols_hbm, cols), ("diff", diff_hbm, diff),
        ("adj", adj_hbm, adj), ("conv", conv_hbm, conv_weight), ("base", base_hbm, base), ("top", top_hbm, top),
    )):
        loads[name] = pltpu.make_async_copy(src, dst, in_sem.at[slot])
        loads[name].start()
    groups = lanes // PACK
    q = n // groups
    me = lax.axis_index("band")
    reg = lax.axis_index("region")
    right = lax.rem(reg + 1, nr)
    left = lax.rem(reg + nr - 1, nr)

    def partner(t):
        d, bit = 0, 1
        while bit < nb:
            d = d + bit * (((me // bit) % 2 + (t // bit) % 2) % 2)
            bit *= 2
        return d

    def to_band(src, dst, s_sem, r_sem, d):
        return pltpu.make_async_remote_copy(
            src_ref=src, dst_ref=dst, send_sem=s_sem, recv_sem=r_sem,
            device_id=(reg, d), device_id_type=pl.DeviceIdType.MESH)

    def to_region(src, dst, s_sem, r_sem, r):
        return pltpu.make_async_remote_copy(
            src_ref=src, dst_ref=dst, send_sem=s_sem, recv_sem=r_sem,
            device_id=(r, me), device_id_type=pl.DeviceIdType.MESH)

    barrier = pltpu.get_barrier_semaphore()
    for t in range(1, nb):
        pl.semaphore_signal(barrier, inc=1, device_id=(reg, partner(t)),
                            device_id_type=pl.DeviceIdType.MESH)
    for r in (left, right):
        pl.semaphore_signal(barrier, inc=1, device_id=(r, me),
                            device_id_type=pl.DeviceIdType.MESH)

    lane_row = lax.broadcasted_iota(jnp.int32, (1, slots), 1)
    eye = (lax.broadcasted_iota(jnp.int32, (slots, slots), 0)
           == lax.broadcasted_iota(jnp.int32, (slots, slots), 1))

    def as_column(row):
        return jnp.sum(jnp.where(eye, row, 0.0), axis=1, keepdims=True)

    for name in ("kern", "xco2", "count"):
        loads[name].wait()

    for d in range(nb):
        w = jnp.where(lane_row < count[0:1, d:d + 1], xco2[0, d:d + 1, :], 0.0)
        ps[d] = as_column(w) * kern[0, d]
    pr[me] = ps[me]

    pl.semaphore_wait(barrier, nb + 1)

    def sounding_copy(t):
        d = partner(t)
        return to_band(ps.at[d], pr.at[me], s_send.at[t], s_recv.at[t], d)

    for t in range(nb - 1, 0, -1):
        sounding_copy(t).start()

    loads["cy"].wait()

    cy_send[0] = cy[pl.ds(jb - 2, lev, stride=jb), :]
    cy_send[1] = cy[pl.ds(jb - 1, lev, stride=jb), :]
    cy_send[2] = cy[pl.ds(0, lev, stride=jb), :]

    def cy_up():
        return to_band(cy_send.at[pl.ds(0, 2)], cy_halo.at[pl.ds(0, 2)], h_send.at[0], h_recv.at[0], me + 1)

    def cy_down():
        return to_band(cy_send.at[pl.ds(2, 1)], cy_halo.at[pl.ds(2, 1)], h_send.at[1], h_recv.at[1], me - 1)

    def mix_up():
        return to_band(mixed.at[pl.ds(jb - 2, 2)], mix_halo.at[pl.ds(0, 2)], h_send.at[2], h_recv.at[2], me + 1)

    def mix_down():
        return to_band(mixed.at[pl.ds(0, 2)], mix_halo.at[pl.ds(2, 2)], h_send.at[3], h_recv.at[3], me - 1)

    has_next = me < nb - 1
    has_prev = me > 0

    @pl.when(has_next)
    def _():
        cy_up().start()

    @pl.when(has_prev)
    def _():
        cy_down().start()

    @pl.when(me == 0)
    def _():
        mix_halo[0:2] = jnp.zeros((2, lev, lanes), F32)
        cy_halo[0:2] = jnp.zeros((2, lev, lanes), F32)

    @pl.when(me == nb - 1)
    def _():
        mix_halo[2:4] = jnp.zeros((2, lev, lanes), F32)
        cy_halo[2:3] = jnp.zeros((1, lev, lanes), F32)

    lane = lax.broadcasted_iota(jnp.int32, (q, lanes), 1)
    lane_in = lane % PACK

    def pack(rows):
        total = jnp.zeros((q, lanes), F32)
        for g in range(groups):
            moved = pltpu.roll(rows(g), (XSTEPS + PACK * g) % lanes, 1)
            total = jnp.where(lane // PACK == g, moved, total)
        return total

    def cx_rows(s, g):
        k, jo = (g * q) // jb, (g * q) % jb
        return cx[k, pl.ds(pl.multiple_of(s * jb + jo, 8), q), :]

    def pack_courant(s, carry):
        cpack[s] = pack(lambda g: cx_rows(s, g))
        return carry

    loads["cx"].wait()
    lax.fori_loop(0, nb, pack_courant, 0)
    c_right = to_region(cpack, cleft, c_send.at[0], c_recv.at[0], right)
    c_left = to_region(cpack, cright, c_send.at[1], c_recv.at[1], left)
    c_right.start()
    c_left.start()

    loads["cols"].wait()
    loads["diff"].wait()

    cell = lax.broadcasted_iota(jnp.int32, (slots, lanes), 1).astype(F32)
    for s in range(nb):
        col = as_column(cols[0, s:s + 1, :].astype(F32))
        for j in range(jb):
            hit = jnp.where(col == cell + float(j * lanes), 1.0, 0.0)
            onehot[s * slots:(s + 1) * slots, j * lanes:(j + 1) * lanes] = hit.astype(BF16)

    def split_mix(j, carry):
        hi, lo = split(diff[j].T)
        dtb[j, :, 0:lev] = hi
        dtb[j, :, lev:2 * lev] = lo
        dtb[j, :, 2 * lev:3 * lev] = hi
        return carry

    lax.fori_loop(0, jb, split_mix, 0)

    for t in range(nb - 1, 0, -1):
        sounding_copy(t).wait_recv()
    for s in range(nb):
        hi, lo = split(pr[s].T)
        ptb[0:lev, s * slots:(s + 1) * slots] = hi
        ptb[lev:2 * lev, s * slots:(s + 1) * slots] = lo

    for name in ("adj", "conv", "base", "top"):
        loads[name].wait()

    level = lax.broadcasted_iota(jnp.int32, (lev, lanes), 0)

    def mix_pair(jp):
        both = jnp.dot(ptb[...], onehot[:, pl.ds(pl.multiple_of(jp * 2 * lanes, 2 * lanes), 2 * lanes)],
                       preferred_element_type=F32)
        add = both[0:lev] + both[lev:2 * lev]
        for h in range(2):
            j = jp * 2 + h
            forced = adj[pl.ds(j, lev, stride=jb), :] + add[:, h * lanes:(h + 1) * lanes]
            lowest, highest = base[pl.ds(j, 1), :], top[pl.ds(j, 1), :]
            inside = (level >= lowest) & (level <= highest)
            depth = (highest - lowest + 1).astype(F32)
            mean = jnp.sum(jnp.where(inside, forced, 0.0), axis=0, keepdims=True) / depth
            conv = forced + jnp.where(inside, conv_weight[pl.ds(j, 1), :] * (mean - forced), 0.0)
            hi, lo = split(conv)
            mixed[j] = jnp.dot(dtb[j], jnp.concatenate([hi, hi, lo], axis=0), preferred_element_type=F32)

    mix_pair(0)

    @pl.when(has_prev)
    def _():
        mix_down().start()

    mix_pair(jb // 2 - 1)

    @pl.when(has_next)
    def _():
        mix_up().start()

    def mix_rest(jp, carry):
        mix_pair(jp)
        return carry

    lax.fori_loop(1, jb // 2 - 1, mix_rest, 0)

    @pl.when(has_next)
    def _():
        cy_down().wait_recv()
        mix_down().wait_recv()

    @pl.when(has_prev)
    def _():
        cy_up().wait_recv()
        mix_up().wait_recv()

    def sweep_y(d, store):
        ls = pl.ds(pl.multiple_of(d * ln, 8), ln)

        def field(r):
            if r < 2:
                return mix_halo[r, ls, :]
            if r < jb + 2:
                return mixed[r - 2, ls, :]
            return mix_halo[r - jb, ls, :]

        def courant(r):
            if r < 2:
                return cy_halo[r, ls, :]
            if r < jb + 2:
                c = cy[pl.ds(d * n + (r - 2), ln, stride=jb), :]
                return jnp.where(has_next, c, 0.0) if r == jb + 1 else c
            return cy_halo[2, ls, :]

        c_prev = jnp.minimum(courant(0), 0.0)
        a_prev, a_here = field(0), field(1)
        b_back = b_here = None
        coef = []
        for r in range(1, jb + 3):
            c_here = courant(r)
            a_next = field(r + 1)
            up = jnp.maximum(c_here, 0.0)
            mid = 1.0 - up + c_prev
            b_next = mid * a_here + up * a_next - c_prev * a_prev
            coef.append((mid, up, c_prev))
            if r >= 3:
                m2, u2, p2 = coef[-2]
                store(r - 3, m2 * b_here + u2 * b_next - p2 * b_back)
            b_back, b_here = b_here, b_next
            a_prev, a_here = a_here, a_next
            c_prev = jnp.minimum(c_here, 0.0)

    def block_copy(t):
        d = partner(t)
        return to_band(outgoing.at[pl.ds(pl.multiple_of(t * n, 8), n)],
                       arrived.at[pl.ds(pl.multiple_of(me * n, 8), n)],
                       a_send.at[t], a_recv.at[t], d)

    def send_block(i, carry):
        t = (i // 2 + 1) + ((i + 1) % 2) * (nb // 2 - 1)

        def store(j, value):
            outgoing[pl.ds(t * n + j, ln, stride=jb), :] = value

        sweep_y(partner(t), store)
        block_copy(t).start()
        return carry

    lax.fori_loop(0, nb - 1, send_block, 0)

    def store_own(j, value):
        arrived[pl.ds(me * n + j, ln, stride=jb), :] = value

    sweep_y(me, store_own)

    def halo_right(t):
        s = partner(t)
        return to_region(xpack.at[s], xleft.at[s], r_send.at[t], r_recv.at[t], right)

    def halo_left(t):
        s = partner(t)
        return to_region(xpack.at[s], xright.at[s], l_send.at[t], l_recv.at[t], left)

    def prepare(t):
        s = partner(t)
        xpack[s] = pack(lambda g: arrived[pl.ds(pl.multiple_of(s * n + g * q, 8), q), :])
        halo_right(t).start()
        halo_left(t).start()

    def finish(t):
        s = partner(t)
        halo_right(t).wait_recv()
        halo_left(t).wait_recv()
        low = lane_in < XSTEPS
        own, c_own = xpack[s], cpack[s]
        a = jnp.where(low, xleft[s], own)
        b = jnp.where(low, own, xright[s])
        ca = jnp.where(low, cleft[s], c_own)
        cb = jnp.where(low, c_own, cright[s])

        def coefs(c):
            up = jnp.maximum(c, 0.0)
            low_prev = pltpu.roll(jnp.minimum(c, 0.0), 1, 1)
            return 1.0 - up + low_prev, up, low_prev

        za, pa, ma = coefs(ca)
        zb, pb, mb = coefs(cb)
        edges = []
        for step in range(XSTEPS):
            a_prev, b_next = pltpu.roll(a, 1, 1), pltpu.roll(b, lanes - 1, 1)
            edges.append(jnp.where(lane_in == XSTEPS, a_prev, b_next))
            if step < XSTEPS - 1:
                a = za * a + pa * pltpu.roll(a, lanes - 1, 1) - ma * a_prev
                b = zb * b + pb * b_next - mb * pltpu.roll(b, 1, 1)
        first, last = lane == 0, lane == lanes - 1
        for g in range(groups):
            back = (lanes - XSTEPS - PACK * g) % lanes
            x = arrived[pl.ds(pl.multiple_of(s * n + g * q, 8), q), :]
            c = cx_rows(s, g)
            up = jnp.maximum(c, 0.0)
            low_prev = jnp.where(first, pltpu.roll(ma, back, 1), pltpu.roll(jnp.minimum(c, 0.0), 1, 1))
            mid = 1.0 - up + low_prev
            for step in range(XSTEPS):
                edge = pltpu.roll(edges[step], back, 1)
                nxt = jnp.where(last, edge, pltpu.roll(x, lanes - 1, 1))
                prv = jnp.where(first, edge, pltpu.roll(x, 1, 1))
                x = mid * x + up * nxt - low_prev * prv
            k, jo = (g * q) // jb, (g * q) % jb
            out[k, pl.ds(pl.multiple_of(s * jb + jo, 8), q), :] = x

    prepare(0)
    for t in range(1, LAG):
        block_copy(t).wait_recv()
        prepare(t)
    c_right.wait_recv()
    c_left.wait_recv()

    def drain(i, carry):
        block_copy(i).wait_recv()
        prepare(i)
        finish(i - LAG)
        return carry

    lax.fori_loop(LAG, nb, drain, 0)

    def finish_rest(t, carry):
        finish(t)
        return carry

    lax.fori_loop(nb - LAG, nb, finish_rest, 0)

    c_right.wait_send()
    c_left.wait_send()

    @pl.when(has_next)
    def _():
        cy_up().wait_send()
        mix_up().wait_send()

    @pl.when(has_prev)
    def _():
        cy_down().wait_send()
        mix_down().wait_send()

    def finish_sends(t, carry):
        halo_right(t).wait_send()
        halo_left(t).wait_send()
        return carry

    lax.fori_loop(0, nb, finish_sends, 0)

    def finish_blocks(t, carry):
        sounding_copy(t).wait_send()
        block_copy(t).wait_send()
        return carry

    lax.fori_loop(1, nb, finish_blocks, 0)


def per_device(nb, nr, adj, cy, cx, diff, conv_weight, base, top, count, xco2, kern, cols):
    lev, jb, lanes = adj.shape
    ln, lat, _ = cx.shape
    slots = kern.shape[2]
    n = ln * jb
    q = n * PACK // lanes
    vmem = pl.BlockSpec(memory_space=pltpu.VMEM)
    hbm = pl.BlockSpec(memory_space=pltpu.HBM)
    operands = (adj.reshape(lev * jb, lanes), cy.reshape(lev * jb, lanes), cx, diff,
                conv_weight, base, top, count, xco2, kern, cols)
    dma = pltpu.SemaphoreType.DMA
    rows = (nb, q, lanes)
    return pl.pallas_call(
        functools.partial(step_kernel, nb, nr, lev, jb, ln, slots),
        out_shape=jax.ShapeDtypeStruct((ln, lat, lanes), F32),
        in_specs=[hbm] * len(operands),
        out_specs=vmem,
        scratch_shapes=[pltpu.VMEM(x.shape, x.dtype) for x in operands] + [
            dma((len(operands),)),
            pltpu.VMEM((nb, slots, lev), F32),
            pltpu.VMEM((nb, slots, lev), F32),
            pltpu.VMEM((nb * slots, jb * lanes), BF16),
            pltpu.VMEM((2 * lev, nb * slots), BF16),
            pltpu.VMEM((jb, lev, 3 * lev), BF16),
            pltpu.VMEM((jb, lev, lanes), F32),
            pltpu.VMEM((4, lev, lanes), F32),
            pltpu.VMEM((3, lev, lanes), F32),
            pltpu.VMEM((3, lev, lanes), F32),
            pltpu.VMEM((nb * n, lanes), F32),
            pltpu.VMEM((nb * n, lanes), F32),
            pltpu.VMEM(rows, F32), pltpu.VMEM(rows, F32), pltpu.VMEM(rows, F32),
            pltpu.VMEM(rows, F32), pltpu.VMEM(rows, F32), pltpu.VMEM(rows, F32),
            dma((nb,)), dma((nb,)), dma((nb,)), dma((nb,)),
            dma((4,)), dma((4,)), dma((2,)), dma((2,)),
            dma((nb,)), dma((nb,)), dma((nb,)), dma((nb,)),
        ],
        compiler_params=pltpu.CompilerParams(
            collective_id=0, has_side_effects=True, vmem_limit_bytes=63 * 1024 * 1024),
    )(*operands)


def solution(mesh):
    in_specs = (
        P(None, "band", "region"),
        P(None, "band", "region"),
        P("band", None, "region"),
        P("band", None, None),
        P("band", "region"),
        P("band", "region"),
        P("band", "region"),
        P("region", "band"),
        P("region", "band", None),
        P("region", "band", None, None),
        P("region", "band", None),
    )
    run = functools.partial(per_device, mesh.shape["band"], mesh.shape["region"])
    return jax.shard_map(
        run, mesh=mesh, in_specs=in_specs, out_specs=P("band", None, "region"), check_vma=False
    )
```
